32 devices in a mesh: layer: 2 (over x), row: 4 (over y, core), col: 4 (over z).
Axes of the slice: x: 2, y: 2, z: 4, core: 2. Of those that a mesh axis runs over, the one named last changes fastest.
Arguments:
- density: bfloat16 [128, 12, 128, 128], P(('layer', 'row', 'col')), as said below
- pattern: int32 [128, 12], P(('layer', 'row', 'col')), may hold values from -1 to 127, as said below
- ham_derivative: bfloat16 [128, 12, 128, 128], P(('layer', 'row', 'col')), may hold values from -0.75 to 0.75
- pair_direction: bfloat16 [3, 128, 12, 1024], P(None, ('layer', 'row', 'col')), may hold values from -1 to 1
- atom_of_group: int32 [4096], P(('layer', 'row', 'col')), may hold values from 0 to 4095, each once
Outputs:
- next_density: bfloat16 [128, 12, 128, 128], P(('layer', 'row', 'col'))
- forces: float32 [3, 4096], P(None, ('layer', 'row', 'col'))
The draws below stay inside these ranges and needn't reach their ends.
Inputs may be any that keep to these rules, and one draw needn't show every extreme that they name: `pattern`: row a lists distinct column blocks, each within 8 blocks of a counted around the 128 blocks in a loop, in rising order of that signed distance; a itself is always listed; unused slots hold -1 and come last; some row uses all 12 slots. `density`: zero in every slot where pattern is -1. `atom_of_group`: each atom is named once.
All inputs are finite; a program needn't handle non-finite values.
Results may differ from the reference program's by a relative error of at most 0.001.
Values may be sent and summed in bfloat16 or wider, within the bound.
No kernel may reach another device: no remote copies, remote signals or barrier semaphores. Data moves between devices by JAX's collectives and lax.ppermute only.
A program may use at most 192 MiB of HBM per device.

```python
import jax
import jax.numpy as jnp
from jax import lax

BLK = 128
KEEP = 12
BROWS = 4
NB = 128
GROUPS = 32
ATOMS = 4096


def kept_columns(key):
    pattern_key = jax.random.fold_in(key, 11)
    reach = 2 * BROWS
    span = 2 * reach + 1
    offsets = jnp.arange(span, dtype=jnp.int32)[None, :]
    score = jax.random.randint(jax.random.fold_in(pattern_key, 1), (NB, span), 0, 1 << 20) * span + offsets
    score = jnp.where(offsets == reach, -1, score)
    rank = jnp.argsort(jnp.argsort(score, axis=1), axis=1)
    counts = jax.random.randint(jax.random.fold_in(pattern_key, 2), (NB,), 2 * KEEP // 3, KEEP + 1)
    counts = counts.at[0].set(KEEP)
    chosen = rank < counts[:, None]
    order_key = jnp.where(chosen, offsets, span + offsets)
    ordered = jnp.sort(order_key, axis=1)[:, :KEEP]
    row_index = jnp.arange(NB, dtype=jnp.int32)[:, None]
    return jnp.where(ordered < span, (row_index + ordered - reach) % NB, -1).astype(jnp.int32)


def draw_pattern(key, part):
    return kept_columns(key)


def draw_density(key, part):
    columns = kept_columns(key)
    value_key = jax.random.fold_in(key, 23)
    shape = (NB, KEEP, BLK, BLK)
    entries = jax.random.normal(value_key, shape)
    kept = (columns >= 0).astype(jnp.float32)[:, :, None, None]
    return (entries * (KEEP * BLK) ** (-0.25) * kept).astype(jnp.bfloat16)


def shard_levels(stream_key, dims, pieces, smallest, high):
    def one(axis_at, shards_of):
        heights = jax.random.uniform(jax.random.fold_in(jax.random.fold_in(stream_key, 6), axis_at), (shards_of,), jnp.float32, smallest / len(pieces), high / len(pieces))
        return jnp.repeat(jnp.exp(heights), dims[axis_at] // shards_of).reshape((-1,) + (1,) * (len(dims) - axis_at - 1))

    loudness = one(*pieces[0])
    for cut in pieces[1:]:
        loudness = loudness * one(*cut)
    return loudness


def scatter_about(own_key, shape, width, limit, split=(), kind=jnp.bfloat16):
    factor_of = shard_levels(own_key, shape, split, -0.22, 0.18) if split else 1.0
    values = jax.random.normal(own_key, shape, jnp.float32) * width * factor_of
    return jnp.minimum(jnp.maximum(values, -limit), limit).astype(kind)


def setup_inputs(seed: int = 0) -> dict:
    key_list = jax.random.split(jax.random.key(seed), 6)
    return {
        "density": draw_density(jax.random.fold_in(key_list[5], 71), 0),
        "pattern": draw_pattern(jax.random.fold_in(key_list[5], 71), 0),
        "ham_derivative": scatter_about(key_list[2], (NB, KEEP, BLK, BLK), (2.0 / (KEEP * BLK) ** 0.5), 0.75, ((0, 32),)),
        "pair_direction": jnp.clip(jax.random.uniform(key_list[3], (3, NB, KEEP, GROUPS * GROUPS), jnp.float32, -1.0, 1.0) * shard_levels(key_list[3], (3, NB, KEEP, GROUPS * GROUPS), ((1, 32),), -0.4, 0.0), -1.0, 1.0).astype(jnp.bfloat16),
        "atom_of_group": jax.random.permutation(key_list[4], ATOMS).astype(jnp.int32),
    }


def one_row(density, pattern, ham_derivative, pair_direction, block_row):
    wanted = pattern[block_row]
    through = jnp.where(wanted >= 0, wanted, block_row).astype(jnp.int32)
    their_slots = pattern[through]
    matches = (their_slots[:, None, :] == wanted[None, :, None]) & (wanted[None, :, None] >= 0)
    slot_index = jnp.sum(jnp.where(matches, jnp.arange(KEEP, dtype=jnp.int32)[None, None, :], 0), axis=2).astype(jnp.int32)
    present = jnp.any(matches, axis=2)
    right_blocks = jnp.where(present[:, :, None, None], density[through[:, None], slot_index], jnp.zeros((), density.dtype))
    left_blocks = density[block_row]
    left_wide = jnp.transpose(left_blocks, (1, 0, 2)).reshape(BLK, KEEP * BLK)
    right_wide = jnp.transpose(right_blocks, (0, 2, 1, 3)).reshape(KEEP * BLK, KEEP * BLK)
    square = jnp.dot(left_wide, right_wide, preferred_element_type=jnp.float32).reshape(BLK, KEEP, BLK).transpose(1, 0, 2)
    widened = left_blocks.astype(jnp.float32)
    mixture = 2.0 * widened - square
    energy = (mixture * ham_derivative[block_row].astype(jnp.float32)).reshape(KEEP, GROUPS, 4, GROUPS, 4).sum(axis=(2, 4))
    pair_factor = pair_direction[:, block_row].astype(jnp.float32).reshape(3, KEEP, GROUPS, GROUPS)
    group_force = jnp.sum(pair_factor * energy[None], axis=(1, 3))
    return mixture.astype(jnp.bfloat16), group_force


def reference(density, pattern, ham_derivative, pair_direction, atom_of_group):
    def visit(block_row):
        return one_row(density, pattern, ham_derivative, pair_direction, block_row)

    next_density, group_force = lax.map(visit, jnp.arange(NB, dtype=jnp.int32))
    flat = jnp.transpose(group_force, (1, 0, 2)).reshape(3, ATOMS)
    forces = jnp.zeros_like(flat).at[:, atom_of_group].set(flat)
    return next_density, forces
```

```python
import functools

import jax
import jax.numpy as jnp
from jax import lax
from jax.experimental import pallas as pl
from jax.experimental.pallas import tpu as pltpu
from jax.sharding import PartitionSpec as P

AXES = ("layer", "row", "col")


def hop(value, distance, keep):
    total = lax.axis_size(AXES)
    line = lax.axis_size("col")
    route = [((i - distance) % total, i) for i in range(total) if keep(i % line)]
    return lax.ppermute(value, AXES, route)


def gathered(block, line):
    up1 = hop(block, 1, lambda z: z >= 1)
    down1 = hop(block, -1, lambda z: z <= line - 2)
    up2 = hop(up1, 1, lambda z: z >= 2)
    down2 = hop(down1, -1, lambda z: z <= line - 3)
    up = {1: up1, 2: up2}
    down = {1: down1, 2: down2}
    for step in range(3, line):
        up[step] = hop(up[step - 1], 1, lambda z, step=step: z >= step)
        down[step] = hop(down[step - 1], -1, lambda z, step=step: z <= line - 1 - step)
    over_far = hop(up[line - 2], -line, lambda z: z >= line - 2)
    over_near = hop(up[line - 1], -line, lambda z: z == line - 1)
    under_far = hop(down[line - 2], line, lambda z: z <= 1)
    under_near = hop(down[line - 1], line, lambda z: z == 0)
    return up1, up2, down1, down2, under_near, under_far, over_near, over_far


def step_kernel(
    rows, keep, where_ref, column_ref, place_ref,
    own, up1, up2, down1, down2, under_near, under_far, over_near, over_far,
    ham_ref, factor_ref,
    next_ref, force_ref,
    held, left, square, product, sems,
):
    size = own.shape[2]
    groups = size // 4
    span = 5 * rows
    batch = rows * keep
    z = place_ref[0]
    line = place_ref[1]

    def fetch(part, near, far, condition):
        spot = held.at[pl.ds(part * batch, batch)]

        @pl.when(condition)
        def _():
            pltpu.make_async_copy(near, spot, sems.at[part]).start()

        if far is not None:

            @pl.when(jnp.logical_not(condition))
            def _():
                pltpu.make_async_copy(far, spot, sems.at[part]).start()

    fetch(2, own, None, z >= 0)
    fetch(1, up1, under_near, z >= 1)
    fetch(3, down1, over_near, z <= line - 2)
    fetch(0, up2, under_far, z >= 2)
    fetch(4, down2, over_far, z <= line - 3)

    held[span * keep] = jnp.zeros((size, size), held.dtype)
    left[...] = jnp.zeros(left.shape, left.dtype)

    def arrived(part):
        spot = held.at[pl.ds(part * batch, batch)]
        pltpu.make_async_copy(own, spot, sems.at[part]).wait()

    arrived(2)
    for i in range(rows):
        for l in range(keep):
            column = column_ref[i, l]

            @pl.when(column >= 0)
            def _(i=i, l=l, column=column):
                at = pl.multiple_of(column * size, size)
                left[i * size : (i + 1) * size, pl.ds(at, size)] = held[2 * batch + i * keep + l]

    for part in (1, 3, 0, 4):
        arrived(part)

    reach = 2 * rows
    for j in range(0, span, 2):
        low, high = max(0, j - reach), min(span, j + 2 + reach)
        right = jnp.concatenate(
            [
                jnp.concatenate([held[where_ref[r, j]], held[where_ref[r, j + 1]]], axis=1)
                for r in range(low, high)
            ],
            axis=0,
        )
        total = jnp.dot(left[:, low * size : high * size], right, preferred_element_type=jnp.float32)
        square[j] = total[:, :size]
        square[j + 1] = total[:, size:]

    for i in range(rows):

        def slot(k, sums, i=i):
            column = column_ref[i, k]
            term = square[jnp.maximum(column, 0), i * size : (i + 1) * size, :]
            term = jnp.where(column >= 0, term, 0.0)
            block = held[2 * batch + i * keep + k].astype(jnp.float32)
            mixture = 2.0 * block - term
            next_ref[i, k] = mixture.astype(next_ref.dtype)
            product[...] = mixture * ham_ref[i, k].astype(jnp.float32)
            energy = product[pl.ds(0, groups, stride=4), :]
            for r in range(1, 4):
                energy = energy + product[pl.ds(r, groups, stride=4), :]
            return tuple(sums[d] + energy * factor_ref[d, i, k].astype(jnp.float32) for d in range(3))

        start = tuple(jnp.zeros((groups, size), jnp.float32) for _ in range(3))
        sums = lax.fori_loop(0, keep, slot, start)
        for d in range(3):
            force_ref[d, i] = sums[d]


def on_device(density, pattern, ham_derivative, pair_direction, atom_of_group):
    rows, keep, size, _ = density.shape
    groups = size // 4
    devices = lax.axis_size(AXES)
    line = lax.axis_size("col")
    blocks = rows * devices
    atoms = blocks * groups
    position = lax.axis_index(AXES)

    patterns = {d: hop(pattern, d, lambda z: True) for d in (2, 1, -1, -2)}
    extended = jnp.concatenate([patterns[2], patterns[1], pattern, patterns[-1], patterns[-2]], axis=0)
    anchor = position * rows - 2 * rows
    span = 5 * rows
    relative = jnp.where(extended >= 0, jnp.mod(extended - anchor, blocks), -1)
    flat_slot = jnp.arange(span * keep, dtype=jnp.int32).reshape(span, keep, 1)
    hit = relative[:, :, None] == jnp.arange(span, dtype=jnp.int32)[None, None, :]
    where = jnp.min(jnp.where(hit, flat_slot, span * keep), axis=1)
    columns = relative[2 * rows : 3 * rows]
    place = jnp.stack([lax.axis_index("col"), jnp.int32(line)]).astype(jnp.int32)

    spread = jnp.repeat(jnp.eye(groups, dtype=jnp.bfloat16), 4, axis=1)
    factor = jnp.dot(pair_direction.reshape(3 * rows * keep * groups, groups), spread)
    factor = factor.reshape(3, rows, keep, groups, size)
    mine = (atom_of_group[:, None] == jnp.arange(atoms, dtype=jnp.int32)[None, :]).astype(jnp.float32)

    near = gathered(density, line)

    any_space = pl.BlockSpec(memory_space=pl.ANY)
    vmem = pl.BlockSpec(memory_space=pltpu.VMEM)
    smem = pl.BlockSpec(memory_space=pltpu.SMEM)
    next_density, sums = pl.pallas_call(
        functools.partial(step_kernel, rows, keep),
        out_shape=(
            jax.ShapeDtypeStruct(density.shape, density.dtype),
            jax.ShapeDtypeStruct((3, rows, groups, size), jnp.float32),
        ),
        in_specs=[smem] * 3 + [any_space] * 9 + [vmem] * 2,
        out_specs=(vmem, vmem),
        scratch_shapes=[
            pltpu.VMEM((span * keep + 1, size, size), jnp.bfloat16),
            pltpu.VMEM((rows * size, span * size), jnp.bfloat16),
            pltpu.VMEM((span, rows * size, size), jnp.float32),
            pltpu.VMEM((size, size), jnp.float32),
            pltpu.SemaphoreType.DMA((5,)),
        ],
        compiler_params=pltpu.CompilerParams(vmem_limit_bytes=48 * 1024 * 1024),
    )(
        where,
        columns,
        place,
        *[x.reshape(rows * keep, size, size) for x in (density, *near)],
        ham_derivative,
        factor,
    )
    flat = jnp.sum(sums, axis=3).reshape(3, rows * groups)
    spread_out = jnp.dot(flat, mine, precision=lax.Precision.HIGHEST)
    pieces = lax.all_to_all(
        spread_out.reshape(3, devices, rows * groups), AXES, split_axis=1, concat_axis=1, tiled=True
    )
    return next_density, jnp.sum(pieces, axis=1)


def solution(mesh):
    spread = P(AXES, None, None, None)
    return jax.shard_map(
        on_device,
        mesh=mesh,
        in_specs=(spread, P(AXES, None), spread, P(None, AXES, None, None), P(AXES)),
        out_specs=(spread, P(None, AXES)),
        check_vma=False,
    )
```

```python
import functools

import jax
import jax.numpy as jnp
from jax import lax
from jax.experimental import pallas as pl
from jax.experimental.pallas import tpu as pltpu
from jax.sharding import PartitionSpec as P

AXES = ("layer", "row", "col")


def fetched(value, offset, keep):
    total = lax.axis_size(AXES)
    line = lax.axis_size("col")
    route = [((i + offset) % total, i) for i in range(total) if keep(i % line)]
    return lax.ppermute(value, AXES, route)


def gathered(parts, line, beside):
    up1 = [fetched(part, -1, lambda z: z >= 1) for part in parts]
    down1 = [fetched(part, 1, lambda z: z <= line - 2) for part in parts]
    up1[-1], down1[-1], beside = lax.optimization_barrier((up1[-1], down1[-1], beside))
    up2 = [fetched(part, -1, lambda z: z >= 2) for part in up1]
    down2 = [fetched(part, 1, lambda z: z <= line - 3) for part in down1]
    brought_up, brought_down = up2, down2
    for step in range(3, line - 1):
        brought_up = [fetched(part, -1, lambda z: z >= step) for part in brought_up]
        brought_down = [fetched(part, 1, lambda z: z <= line - 1 - step) for part in brought_down]
    over_near = [fetched(part, line - 1, lambda z: z == line - 1) for part in brought_up]
    under_near = [fetched(part, 1 - line, lambda z: z == 0) for part in brought_down]
    over_far = [fetched(part, line, lambda z: z >= line - 2) for part in brought_up]
    under_far = [fetched(part, -line, lambda z: z <= 1) for part in brought_down]
    return [up1, up2, down1, down2, under_near, under_far, over_near, over_far], beside


def step_kernel(rows, keep, cuts, where_ref, column_ref, place_ref, own, *refs):
    others, (ham_ref, factor_ref, next_ref, force_ref), (held, left, square, product, sems) = (
        refs[: 8 * cuts], refs[8 * cuts : -5][:4], refs[-5:],
    )
    others = [others[g * cuts : (g + 1) * cuts] for g in range(8)]
    up1, up2, down1, down2, under_near, under_far, over_near, over_far = others
    size = own.shape[2]
    groups = size // 4
    span = 5 * rows
    batch = rows * keep
    piece = batch // cuts
    z = place_ref[0]
    line = place_ref[1]

    def fetch(part, here, there, condition):
        @pl.when(condition)
        def _():
            for h in range(cuts):
                spot = held.at[pl.ds(part * batch + h * piece, piece)]
                pltpu.make_async_copy(here[h], spot, sems.at[part]).start()

        @pl.when(jnp.logical_not(condition))
        def _():
            for h in range(cuts):
                spot = held.at[pl.ds(part * batch + h * piece, piece)]
                pltpu.make_async_copy(there[h], spot, sems.at[part]).start()

    pltpu.make_async_copy(own, held.at[pl.ds(2 * batch, batch)], sems.at[2]).start()
    fetch(1, up1, under_near, z >= 1)
    fetch(3, down1, over_near, z <= line - 2)
    fetch(0, up2, under_far, z >= 2)
    fetch(4, down2, over_far, z <= line - 3)

    held[span * keep] = jnp.zeros((size, size), held.dtype)
    left[...] = jnp.zeros(left.shape, left.dtype)

    def arrived(part):
        spot = held.at[pl.ds(part * batch, batch)]
        pltpu.make_async_copy(own, spot, sems.at[part]).wait()

    arrived(2)
    for i in range(rows):
        for l in range(keep):
            column = column_ref[i, l]

            @pl.when(column >= 0)
            def _(i=i, l=l, column=column):
                at = pl.multiple_of(column * size, size)
                left[i * size : (i + 1) * size, pl.ds(at, size)] = held[2 * batch + i * keep + l]

    for part in (1, 3, 0, 4):
        arrived(part)

    reach = 2 * rows
    for j in range(0, span, 2):
        low, high = max(0, j - reach), min(span, j + 2 + reach)
        right = jnp.concatenate(
            [
                jnp.concatenate([held[where_ref[r, j]], held[where_ref[r, j + 1]]], axis=1)
                for r in range(low, high)
            ],
            axis=0,
        )
        total = jnp.dot(left[:, low * size : high * size], right, preferred_element_type=jnp.float32)
        square[j] = total[:, :size]
        square[j + 1] = total[:, size:]

    for i in range(rows):

        def slot(k, sums, i=i):
            column = column_ref[i, k]
            term = square[jnp.maximum(column, 0), i * size : (i + 1) * size, :]
            term = jnp.where(column >= 0, term, 0.0)
            block = held[2 * batch + i * keep + k].astype(jnp.float32)
            mixture = 2.0 * block - term
            next_ref[i, k] = mixture.astype(next_ref.dtype)
            product[...] = mixture * ham_ref[i, k].astype(jnp.float32)
            energy = product[pl.ds(0, groups, stride=4), :]
            for r in range(1, 4):
                energy = energy + product[pl.ds(r, groups, stride=4), :]
            return tuple(sums[d] + energy * factor_ref[d, i, k].astype(jnp.float32) for d in range(3))

        start = tuple(jnp.zeros((groups, size), jnp.float32) for _ in range(3))
        sums = lax.fori_loop(0, keep, slot, start)
        for d in range(3):
            force_ref[d, i] = sums[d]


def on_device(density, pattern, ham_derivative, pair_direction, atom_of_group):
    rows, keep, size, _ = density.shape
    groups = size // 4
    devices = lax.axis_size(AXES)
    line = lax.axis_size("col")
    blocks = rows * devices
    atoms = blocks * groups
    position = lax.axis_index(AXES)

    cuts = 2
    piece = rows // cuts
    patterns = {d: fetched(pattern, d, lambda z: True) for d in (-2, -1, 1, 2)}
    parts = [density[h * piece : (h + 1) * piece] for h in range(cuts)]
    parts, patterns = lax.optimization_barrier((parts, patterns))
    extended = jnp.concatenate([patterns[-2], patterns[-1], pattern, patterns[1], patterns[2]], axis=0)
    anchor = position * rows - 2 * rows
    span = 5 * rows
    relative = jnp.where(extended >= 0, jnp.mod(extended - anchor, blocks), -1)
    flat_slot = jnp.arange(span * keep, dtype=jnp.int32).reshape(span, keep, 1)
    hit = relative[:, :, None] == jnp.arange(span, dtype=jnp.int32)[None, None, :]
    where = jnp.min(jnp.where(hit, flat_slot, span * keep), axis=1)
    columns = relative[2 * rows : 3 * rows]
    place = jnp.stack([lax.axis_index("col"), jnp.int32(line)]).astype(jnp.int32)

    spread = jnp.repeat(jnp.eye(groups, dtype=jnp.bfloat16), 4, axis=1)
    factor = jnp.dot(pair_direction.reshape(3 * rows * keep * groups, groups), spread)
    factor = factor.reshape(3, rows, keep, groups, size)
    mine = (atom_of_group[:, None] == jnp.arange(atoms, dtype=jnp.int32)[None, :]).astype(jnp.float32)

    near, (where, columns, factor) = gathered(parts, line, (where, columns, factor))
    near = [part.reshape(piece * keep, size, size) for parts in near for part in parts]

    any_space = pl.BlockSpec(memory_space=pl.ANY)
    vmem = pl.BlockSpec(memory_space=pltpu.VMEM)
    smem = pl.BlockSpec(memory_space=pltpu.SMEM)
    next_density, sums = pl.pallas_call(
        functools.partial(step_kernel, rows, keep, cuts),
        out_shape=(
            jax.ShapeDtypeStruct(density.shape, density.dtype),
            jax.ShapeDtypeStruct((3, rows, groups, size), jnp.float32),
        ),
        in_specs=[smem] * 3 + [any_space] * (1 + len(near)) + [vmem] * 2,
        out_specs=(vmem, vmem),
        scratch_shapes=[
            pltpu.VMEM((span * keep + 1, size, size), jnp.bfloat16),
            pltpu.VMEM((rows * size, span * size), jnp.bfloat16),
            pltpu.VMEM((span, rows * size, size), jnp.float32),
            pltpu.VMEM((size, size), jnp.float32),
            pltpu.SemaphoreType.DMA((5,)),
        ],
        compiler_params=pltpu.CompilerParams(vmem_limit_bytes=48 * 1024 * 1024),
    )(
        where,
        columns,
        place,
        density.reshape(rows * keep, size, size),
        *near,
        ham_derivative,
        factor,
    )
    flat = jnp.sum(sums, axis=3).reshape(3, rows * groups)
    spread_out = jnp.dot(flat, mine, precision=lax.Precision.HIGHEST)
    pieces = lax.all_to_all(
        spread_out.reshape(3, devices, rows * groups), AXES, split_axis=1, concat_axis=1, tiled=True
    )
    return next_density, jnp.sum(pieces, axis=1)


def solution(mesh):
    spread = P(AXES, None, None, None)
    return jax.shard_map(
        on_device,
        mesh=mesh,
        in_specs=(spread, P(AXES, None), spread, P(None, AXES, None, None), P(AXES)),
        out_specs=(spread, P(None, AXES)),
        check_vma=False,
    )
```

```python
import functools

import jax
import jax.numpy as jnp
from jax import lax
from jax.experimental import pallas as pl
from jax.experimental.pallas import tpu as pltpu
from jax.sharding import PartitionSpec as P

AXES = ("layer", "row", "col")
UNUSED = 64
TAIL = 16


def fetched(value, offset, keep):
    total = lax.axis_size(AXES)
    line = lax.axis_size("col")
    route = [((i + offset) % total, i) for i in range(total) if keep(i % line)]
    return lax.ppermute(value, AXES, route)


def early_kernel(rows, keep, where_ref, column_ref, place_ref, own, *refs):
    near, (mixture_out, late_out, held, left, square, mixture_ref, late_ref, sems, out_sems) = refs[:8], refs[8:]
    near = [near[g : g + 2] for g in range(0, 8, 2)]
    size = own.shape[1]
    span = 5 * rows
    height = rows * keep * size
    half = height // 2
    z = place_ref[0]
    line = place_ref[1]
    sources = (
        (0, near[1], z >= 2),
        (1, near[0], z >= 1),
        (3, near[2], z <= line - 2),
        (4, near[3], z <= line - 3),
    )

    def copies(part, pair):
        return [
            pltpu.make_async_copy(
                pair[h].at[pl.ds(0, half)],
                held.at[pl.ds(part * height + h * half, half)],
                sems.at[part, h],
            )
            for h in range(2)
        ]

    mine = pltpu.make_async_copy(own, held.at[pl.ds(2 * height, height)], sems.at[2, 0])
    mine.start()
    for part, pair, valid in sources:

        @pl.when(valid)
        def _(part=part, pair=pair):
            for copy in copies(part, pair):
                copy.start()

    held[pl.ds(5 * height, size)] = jnp.zeros((size, size), held.dtype)
    left[...] = jnp.zeros(left.shape, left.dtype)
    mine.wait()
    for i in range(rows):
        for l in range(keep):
            column = column_ref[i, l]

            @pl.when(column >= 0)
            def _(i=i, l=l, column=column):
                at = pl.multiple_of(column * size, size)
                block = held[pl.ds(2 * height + (i * keep + l) * size, size)]
                left[i * size : (i + 1) * size, pl.ds(at, size)] = block

    width = late_ref.shape[1]
    start = pl.multiple_of(jnp.where(z <= 1, 0, span * size - width), size)
    late_ref[...] = left[:, pl.ds(start, width)]
    put_left = pltpu.make_async_copy(late_ref, late_out, out_sems.at[rows])
    put_left.start()
    for part, pair, valid in sources:

        @pl.when(valid)
        def _(part=part, pair=pair):
            for copy in copies(part, pair):
                copy.wait()

    reach = 2 * rows
    for j in range(0, span, 2):
        low, high = max(0, j - reach), min(span, j + 2 + reach)

        def block(r, c):
            return held[pl.ds(pl.multiple_of(where_ref[r, c] * size, size), size)]

        right = jnp.concatenate(
            [jnp.concatenate([block(r, j), block(r, j + 1)], axis=1) for r in range(low, high)], axis=0
        )
        total = jnp.dot(left[:, low * size : high * size], right, preferred_element_type=jnp.float32)
        square[j] = total[:, :size]
        square[j + 1] = total[:, size:]

    put_mixture = []
    for i in range(rows):

        @pl.loop(0, keep)
        def _(k, i=i):
            column = column_ref[i, k]
            term = square[jnp.maximum(column, 0), i * size : (i + 1) * size, :]
            term = jnp.where(column >= 0, term, 0.0)
            at = pl.multiple_of(2 * height + (i * keep + k) * size, size)
            mixture_ref[i, k] = 2.0 * held[pl.ds(at, size)].astype(jnp.float32) - term

        put_mixture.append(pltpu.make_async_copy(mixture_ref.at[i], mixture_out.at[i], out_sems.at[i]))
        put_mixture[i].start()
    put_left.wait()
    for put in put_mixture:
        put.wait()


def late_kernel(rows, keep, where_ref, column_ref, place_ref, *refs):
    left_in, near_a, near_b, far_a, far_b, mixture_in, ham_in, factor_in, next_out, force_ref = refs[:10]
    left, held, mixture_ref, ham_ref, factor_ref, next_ref, square, product, sems, out_sems = refs[10:]
    size = ham_ref.shape[2]
    groups = size // 4
    span = 5 * rows
    reach = 2 * rows
    height = rows * keep * size
    half = height // 2
    low = place_ref[0] <= 1
    near_at = pl.multiple_of(jnp.where(low, height, 0), size)
    far_at = pl.multiple_of(jnp.where(low, 0, height), size)
    routes = [(left_in, left)]
    for there, at in ((far_a, far_at), (near_a, near_at), (far_b, far_at + half), (near_b, near_at + half)):
        routes.append((there.at[pl.ds(0, half)], held.at[pl.ds(pl.multiple_of(at, size), half)]))
    routes += [(mixture_in, mixture_ref), (ham_in, ham_ref), (factor_in, factor_ref)]
    gets = [pltpu.make_async_copy(there, here, sems.at[n]) for n, (there, here) in enumerate(routes)]
    for get in gets:
        get.start()
    held[pl.ds(2 * height, size)] = jnp.zeros((size, size), held.dtype)
    for get in gets[:5]:
        get.wait()

    def block(r, c):
        return held[pl.ds(pl.multiple_of(where_ref[r, c] * size, size), size)]

    for j in range(0, 2 * reach, 2):
        right = jnp.concatenate(
            [jnp.concatenate([block(r, j), block(r, j + 1)], axis=1) for r in range(reach)], axis=0
        )
        total = jnp.dot(left[...], right, preferred_element_type=jnp.float32)
        square[j] = total[:, :size]
        square[j + 1] = total[:, size:]

    for get in gets[5:]:
        get.wait()
    offset = jnp.where(low, 0, span - 2 * reach)
    puts = []
    for i in range(rows):

        def slot(k, sums, i=i):
            column = column_ref[i, k]
            place = column - offset
            inside = (column >= 0) & (place >= 0) & (place < 2 * reach)
            term = square[jnp.where(inside, place, 0), i * size : (i + 1) * size, :]
            mixture = mixture_ref[i, k] - jnp.where(inside, term, 0.0)
            next_ref[i, k] = mixture.astype(next_ref.dtype)
            product[...] = mixture * ham_ref[i, k].astype(jnp.float32)
            energy = product[pl.ds(0, groups, stride=4), :]
            for r in range(1, 4):
                energy = energy + product[pl.ds(r, groups, stride=4), :]
            return tuple(sums[d] + energy * factor_ref[d, i, k].astype(jnp.float32) for d in range(3))

        start = tuple(jnp.zeros((groups, size), jnp.float32) for _ in range(3))
        sums = lax.fori_loop(0, keep, slot, start)
        puts.append(pltpu.make_async_copy(next_ref.at[i], next_out.at[i], out_sems.at[i]))
        puts[i].start()
        for d in range(3):
            force_ref[d, i] = sums[d]
    for put in puts:
        put.wait()


def on_device(density, pattern, ham_derivative, pair_direction, atom_of_group):
    rows, keep, size, _ = density.shape
    groups = size // 4
    devices = lax.axis_size(AXES)
    line = lax.axis_size("col")
    blocks = rows * devices
    atoms = blocks * groups
    reach = 2 * rows
    span = 5 * rows
    position = lax.axis_index(AXES)
    z = lax.axis_index("col")

    row_at = jnp.arange(span, dtype=jnp.int32)[:, None]
    distance = jnp.mod(pattern - (position * rows + row_at[:rows]) + reach, blocks) - reach
    distance = jnp.where(pattern >= 0, distance, UNUSED)
    tail = jnp.pad(distance.astype(jnp.bfloat16), ((0, TAIL - rows), (0, size - keep)))

    flat = density.reshape(rows * keep * size, size)
    half = rows * keep * size // 2
    parts = [jnp.concatenate([flat[:half], tail], axis=0), jnp.pad(flat[half:], ((0, 2 * TAIL), (0, 0)))]

    def columns_of(pieces):
        return jnp.concatenate([x[half : half + rows, :keep].astype(jnp.int32) for x in pieces], axis=0)

    def steps(part):
        up1 = fetched(part, -1, lambda z: z >= 1)
        down1 = fetched(part, 1, lambda z: z <= line - 2)
        up2 = fetched(up1, -1, lambda z: z >= 2)
        down2 = fetched(down1, 1, lambda z: z <= line - 3)
        brought_up, brought_down = up2, down2
        for step in range(3, line - 1):
            brought_up = fetched(brought_up, -1, lambda z: z >= step)
            brought_down = fetched(brought_down, 1, lambda z: z <= line - 1 - step)
        brought = jnp.where(z >= line - 2, brought_up, brought_down)
        total = line * lax.axis_size(("layer", "row"))
        over = [((i + line - 1) % total, i) for i in range(total) if i % line == line - 1]
        under = [((i + 1 - line) % total, i) for i in range(total) if i % line == 0]
        near = lax.ppermute(brought, AXES, over + under)
        over = [((i + line) % total, i) for i in range(total) if i % line >= line - 2]
        under = [((i - line) % total, i) for i in range(total) if i % line <= 1]
        far = lax.ppermute(brought, AXES, over + under)
        return (up1, up2, down1, down2), near, far

    line_a, near_a, far_a = steps(parts[0])
    line_b, near_b, far_b = steps(parts[1])

    group = row_at // rows
    known = ((group != 0) | (z >= 2)) & ((group != 1) | (z >= 1))
    known = known & ((group != 3) | (z <= line - 2)) & ((group != 4) | (z <= line - 3))
    up, down = columns_of([line_a[1], line_a[0]]), columns_of(line_a[2:])
    extended = jnp.concatenate([up, distance, down], axis=0)
    extended = jnp.where(known & (extended != UNUSED), extended + row_at, -1)
    hit = extended[:, :, None] == jnp.arange(span, dtype=jnp.int32)[None, None, :]
    flat_slot = jnp.arange(span * keep, dtype=jnp.int32).reshape(span, keep, 1)
    where_early = jnp.min(jnp.where(hit, flat_slot, span * keep), axis=1)
    columns = jnp.where(distance != UNUSED, distance + reach + row_at[:rows], -1)

    low = z <= 1
    late = columns_of([far_a, near_a, far_a])
    late = jnp.where(low, late[:reach], late[rows : rows + reach])
    group = row_at[:reach] // rows
    known = jnp.where(low, (group == 0) | (z == 0), jnp.where(group == 0, z == line - 1, z >= line - 2))
    first = jnp.where(low, 0, reach)
    late = jnp.where(known & (late != UNUSED), late + first + row_at[:reach], -1)
    hit = late[:, :, None] == jnp.arange(2 * reach, dtype=jnp.int32)[None, None, :]
    where_late = jnp.min(jnp.where(hit, flat_slot[:reach], reach * keep), axis=1)
    place = jnp.stack([z, jnp.int32(line)]).astype(jnp.int32)

    spread = jnp.repeat(jnp.eye(groups, dtype=jnp.bfloat16), 4, axis=1)
    factor = jnp.dot(pair_direction.reshape(3 * rows * keep * groups, groups), spread)
    factor = factor.reshape(3, rows, keep, groups, size)

    hbm = pl.BlockSpec(memory_space=pltpu.HBM)
    vmem = pl.BlockSpec(memory_space=pltpu.VMEM)
    smem = pl.BlockSpec(memory_space=pltpu.SMEM)
    limit = pltpu.CompilerParams(vmem_limit_bytes=60 * 1024 * 1024)
    mixture, left = pl.pallas_call(
        functools.partial(early_kernel, rows, keep),
        out_shape=(
            jax.ShapeDtypeStruct(density.shape, jnp.float32),
            jax.ShapeDtypeStruct((rows * size, reach * size), jnp.bfloat16),
        ),
        in_specs=[smem] * 3 + [hbm] * 9,
        out_specs=(hbm, hbm),
        scratch_shapes=[
            pltpu.VMEM(((span * keep + 1) * size, size), jnp.bfloat16),
            pltpu.VMEM((rows * size, span * size), jnp.bfloat16),
            pltpu.VMEM((span, rows * size, size), jnp.float32),
            pltpu.VMEM(density.shape, jnp.float32),
            pltpu.VMEM((rows * size, reach * size), jnp.bfloat16),
            pltpu.SemaphoreType.DMA((5, 2)),
            pltpu.SemaphoreType.DMA((rows + 1,)),
        ],
        compiler_params=limit,
        name="early",
    )(where_early, columns, place, flat, *[x for pair in zip(line_a, line_b) for x in pair])
    next_density, sums = pl.pallas_call(
        functools.partial(late_kernel, rows, keep),
        out_shape=(
            jax.ShapeDtypeStruct(density.shape, density.dtype),
            jax.ShapeDtypeStruct((3, rows, groups, size), jnp.float32),
        ),
        in_specs=[smem] * 3 + [hbm] * 8,
        out_specs=(hbm, vmem),
        scratch_shapes=[
            pltpu.VMEM(left.shape, left.dtype),
            pltpu.VMEM(((reach * keep + 1) * size, size), jnp.bfloat16),
            pltpu.VMEM(mixture.shape, mixture.dtype),
            pltpu.VMEM(ham_derivative.shape, ham_derivative.dtype),
            pltpu.VMEM(factor.shape, factor.dtype),
            pltpu.VMEM(density.shape, density.dtype),
            pltpu.VMEM((2 * reach, rows * size, size), jnp.float32),
            pltpu.VMEM((size, size), jnp.float32),
            pltpu.SemaphoreType.DMA((8,)),
            pltpu.SemaphoreType.DMA((rows,)),
        ],
        compiler_params=limit,
        name="late",
    )(where_late, columns, place, left, near_a, near_b, far_a, far_b, mixture, ham_derivative, factor)
    force = jnp.sum(sums, axis=3).reshape(3, rows * groups)
    mine = (atom_of_group[:, None] == jnp.arange(atoms, dtype=jnp.int32)[None, :]).astype(jnp.float32)
    spread_out = jnp.dot(force, mine, precision=lax.Precision.HIGHEST)
    pieces = lax.all_to_all(
        spread_out.reshape(3, devices, rows * groups), AXES, split_axis=1, concat_axis=1, tiled=True
    )
    return next_density, jnp.sum(pieces, axis=1)


def solution(mesh):
    spread = P(AXES, None, None, None)
    return jax.shard_map(
        on_device,
        mesh=mesh,
        in_specs=(spread, P(AXES, None), spread, P(None, AXES, None, None), P(AXES)),
        out_specs=(spread, P(None, AXES)),
        check_vma=False,
    )
```

```python
import functools

import jax
import jax.numpy as jnp
from jax import lax
from jax.experimental import pallas as pl
from jax.experimental.pallas import tpu as pltpu
from jax.sharding import PartitionSpec as P

AXES = ("layer", "row", "col")
UNUSED = 64
TAIL = 16


def fetched(value, offset, keep):
    total = lax.axis_size(AXES)
    line = lax.axis_size("col")
    route = [((i + offset) % total, i) for i in range(total) if keep(i % line)]
    return lax.ppermute(value, AXES, route)


def pack_kernel(rows, blocks, pattern_ref, flat, first, second, wide, sems):
    half = flat.shape[0] // 2
    position = lax.axis_index(AXES)
    copies = [
        pltpu.make_async_copy(flat.at[pl.ds(n * half, half)], part.at[pl.ds(0, half)], sems.at[n])
        for n, part in enumerate((first, second))
    ]
    for copy in copies:
        copy.start()
    pattern = pattern_ref[...]
    reach = 2 * rows
    row = position * rows + lax.broadcasted_iota(jnp.int32, pattern.shape, 0)
    distance = lax.rem(pattern - row + (reach + blocks), blocks) - reach
    distance = jnp.where(pattern >= 0, distance, UNUSED)
    wide[...] = jnp.zeros_like(wide)
    wide[: pattern.shape[0], : pattern.shape[1]] = distance.astype(jnp.float32)
    first[pl.ds(half, TAIL)] = wide[...].astype(first.dtype)
    second[pl.ds(half, 2 * TAIL)] = jnp.zeros((2 * TAIL, second.shape[1]), second.dtype)
    for copy in copies:
        copy.wait()


def early_kernel(rows, keep, where_ref, column_ref, place_ref, own, *refs):
    near, (mixture_out, late_out, held, left, square, mixture_ref, late_ref, sems, out_sems) = refs[:8], refs[8:]
    near = [near[g : g + 2] for g in range(0, 8, 2)]
    size = own.shape[1]
    span = 5 * rows
    height = rows * keep * size
    half = height // 2
    z = place_ref[0]
    line = place_ref[1]
    sources = (
        (0, near[1], z >= 2),
        (1, near[0], z >= 1),
        (3, near[2], z <= line - 2),
        (4, near[3], z <= line - 3),
    )

    def copies(part, pair):
        return [
            pltpu.make_async_copy(
                pair[h].at[pl.ds(0, half)],
                held.at[pl.ds(part * height + h * half, half)],
                sems.at[part, h],
            )
            for h in range(2)
        ]

    mine = pltpu.make_async_copy(own, held.at[pl.ds(2 * height, height)], sems.at[2, 0])
    mine.start()
    for part, pair, valid in sources:

        @pl.when(valid)
        def _(part=part, pair=pair):
            for copy in copies(part, pair):
                copy.start()

    held[pl.ds(5 * height, size)] = jnp.zeros((size, size), held.dtype)
    left[...] = jnp.zeros(left.shape, left.dtype)
    mine.wait()
    for i in range(rows):
        for l in range(keep):
            column = column_ref[i, l]

            @pl.when(column >= 0)
            def _(i=i, l=l, column=column):
                at = pl.multiple_of(column * size, size)
                block = held[pl.ds(2 * height + (i * keep + l) * size, size)]
                left[i * size : (i + 1) * size, pl.ds(at, size)] = block

    width = late_ref.shape[2] // 2
    start = jnp.where(z <= 1, 0, span * size - 4 * width)
    for h in range(2):
        for part in range(2):
            at = pl.multiple_of(start + (2 * part + h) * width, size)
            late_ref[h, :, part * width : (part + 1) * width] = left[:, pl.ds(at, width)]
    put_left = pltpu.make_async_copy(late_ref, late_out, out_sems.at[rows])
    put_left.start()
    for part, pair, valid in sources:

        @pl.when(valid)
        def _(part=part, pair=pair):
            for copy in copies(part, pair):
                copy.wait()

    reach = 2 * rows
    for j in range(0, span, 2):
        low, high = max(0, j - reach), min(span, j + 2 + reach)

        def block(r, c):
            return held[pl.ds(pl.multiple_of(where_ref[r, c] * size, size), size)]

        right = jnp.concatenate(
            [jnp.concatenate([block(r, j), block(r, j + 1)], axis=1) for r in range(low, high)], axis=0
        )
        total = jnp.dot(left[:, low * size : high * size], right, preferred_element_type=jnp.float32)
        square[j] = total[:, :size]
        square[j + 1] = total[:, size:]

    put_mixture = []
    for i in range(rows):

        @pl.loop(0, keep, unroll=True)
        def _(k, i=i):
            column = column_ref[i, k]
            term = square[jnp.maximum(column, 0), i * size : (i + 1) * size, :]
            term = jnp.where(column >= 0, term, 0.0)
            at = pl.multiple_of(2 * height + (i * keep + k) * size, size)
            mixture_ref[i, k] = 2.0 * held[pl.ds(at, size)].astype(jnp.float32) - term

        put_mixture.append(pltpu.make_async_copy(mixture_ref.at[i], mixture_out.at[i], out_sems.at[i]))
        put_mixture[i].start()
    put_left.wait()
    for put in put_mixture:
        put.wait()


def late_terms(rows, keep, half, where_ref, place_ref, given, left, held, square, sems):
    left_in, near, far = given
    size = held.shape[1]
    reach = 2 * rows
    count = reach * keep * size // 4
    low = place_ref[0] <= 1
    near_at = pl.multiple_of(jnp.where(low, count, 0), size)
    far_at = pl.multiple_of(jnp.where(low, 0, count), size)
    gets = [
        pltpu.make_async_copy(far.at[pl.ds(0, count)], held.at[pl.ds(far_at, count)], sems.at[1]),
        pltpu.make_async_copy(near.at[pl.ds(0, count)], held.at[pl.ds(near_at, count)], sems.at[2]),
    ]
    if left_in is not None:
        gets.append(pltpu.make_async_copy(left_in.at[half], left, sems.at[0]))
    for get in gets:
        get.start()
    held[pl.ds(2 * count, size)] = jnp.zeros((size, size), held.dtype)

    def block(r, c):
        return held[pl.ds(pl.multiple_of(where_ref[r, c] * size, size), size)]

    def finish():
        for get in gets:
            get.wait()
        span = [part * rows + half * rows // 2 + n for part in range(2) for n in range(rows // 2)]
        for j in range(0, 2 * reach, 2):
            right = jnp.concatenate(
                [jnp.concatenate([block(r, j), block(r, j + 1)], axis=1) for r in span], axis=0
            )
            total = jnp.dot(left[...], right, preferred_element_type=jnp.float32)
            square[j] = total[:, :size]
            square[j + 1] = total[:, size:]

    def term(column, i):
        place = column - jnp.where(low, 0, rows)
        inside = (column >= 0) & (place >= 0) & (place < 2 * reach)
        value = square[jnp.where(inside, place, 0), i * size : (i + 1) * size, :]
        return jnp.where(inside, value, 0.0)

    return finish, term


def middle_kernel(
    rows, keep, where_ref, column_ref, place_ref, left_in, near, far, mixture_in, ham_in, factor_in, mine_in,
    mixture_ref, ham, factor, mine, left_out,
    left, held, square, sems, row_sems,
):
    given = (left_in, near, far)
    finish, term = late_terms(rows, keep, 0, where_ref, place_ref, given, left, held, square, sems)
    gets = [pltpu.make_async_copy(mixture_in.at[i], mixture_ref.at[i], row_sems.at[i]) for i in range(rows)]
    kept = [(ham_in, ham), (factor_in, factor), (mine_in, mine), (left_in.at[1], left_out)]
    others = [
        pltpu.make_async_copy(there, here, row_sems.at[rows + n]) for n, (there, here) in enumerate(kept)
    ]
    for get in gets + others:
        get.start()
    finish()
    for i in range(rows):
        gets[i].wait()

        @pl.loop(0, keep, unroll=True)
        def _(k, i=i):
            mixture_ref[i, k] = mixture_ref[i, k] - term(column_ref[i, k], i)

    for get in others:
        get.wait()


def late_kernel(
    rows, keep, where_ref, column_ref, place_ref, near, far, mixture_ref, ham_ref, factor_ref, mine, left,
    next_out, force_ref,
    held, next_ref, square, product, sums_ref, sems, out_sems,
):
    given = (None, near, far)
    finish, term = late_terms(rows, keep, 1, where_ref, place_ref, given, left, held, square, sems)
    size = ham_ref.shape[2]
    groups = size // 4
    puts = [pltpu.make_async_copy(next_ref.at[i], next_out.at[i], out_sems.at[i]) for i in range(rows)]
    finish()
    for i in range(rows):

        def slot(k, sums, i=i):
            mixture = mixture_ref[i, k] - term(column_ref[i, k], i)
            next_ref[i, k] = mixture.astype(next_ref.dtype)
            product[...] = mixture * ham_ref[i, k].astype(jnp.float32)
            energy = product[pl.ds(0, groups, stride=4), :]
            for r in range(1, 4):
                energy = energy + product[pl.ds(r, groups, stride=4), :]
            return tuple(sums[d] + energy * factor_ref[d, i, k].astype(jnp.float32) for d in range(3))

        start = tuple(jnp.zeros((groups, size), jnp.float32) for _ in range(3))
        sums = lax.fori_loop(0, keep, slot, start, unroll=True)
        puts[i].start()
        for d in range(3):
            sums_ref[d, i * groups : (i + 1) * groups] = sums[d]

    def split(value):
        high = value.astype(jnp.bfloat16)
        rest = value - high.astype(jnp.float32)
        middle = rest.astype(jnp.bfloat16)
        low = (rest - middle.astype(jnp.float32)).astype(jnp.bfloat16)
        return high, middle, low

    ones = jnp.ones((8, size), jnp.bfloat16)
    line = lax.broadcasted_iota(jnp.int32, (8, rows * groups), 0)
    force = jnp.zeros((8, rows * groups), jnp.float32)
    for d in range(3):
        total = sum(
            lax.dot_general(ones, part, (((1,), (1,)), ((), ())), preferred_element_type=jnp.float32)
            for part in split(sums_ref[d])
        )
        force = jnp.where(line == d, total, force)
    parts = jnp.concatenate([part.astype(jnp.float32) for part in split(force)], axis=0).astype(jnp.bfloat16)
    own_atoms = force_ref.shape[2]
    batch = 8
    for put in puts:
        put.wait()

    def place(n, carry):
        at = pl.multiple_of(n * batch * own_atoms, own_atoms)
        placed = jnp.dot(parts, mine[:, pl.ds(at, batch * own_atoms)], preferred_element_type=jnp.float32)
        placed = placed[:8] + placed[8:16] + placed[16:]
        for e in range(batch):
            force_ref[n * batch + e] = placed[:3, e * own_atoms : (e + 1) * own_atoms]
        return carry

    lax.fori_loop(0, force_ref.shape[0] // batch, place, 0, unroll=True if force_ref.shape[0] <= 64 else 1)


def on_device(density, pattern, ham_derivative, pair_direction, atom_of_group):
    rows, keep, size, _ = density.shape
    groups = size // 4
    devices = lax.axis_size(AXES)
    line = lax.axis_size("col")
    blocks = rows * devices
    atoms = blocks * groups
    reach = 2 * rows
    span = 5 * rows
    position = lax.axis_index(AXES)
    z = lax.axis_index("col")

    row_at = jnp.arange(span, dtype=jnp.int32)[:, None]
    distance = jnp.mod(pattern - (position * rows + row_at[:rows]) + reach, blocks) - reach
    distance = jnp.where(pattern >= 0, distance, UNUSED)
    flat = density.reshape(rows * keep * size, size)
    half = rows * keep * size // 2
    parts = pl.pallas_call(
        functools.partial(pack_kernel, rows, blocks),
        out_shape=[pltpu.VMEM((half + n, size), density.dtype) for n in (TAIL, 2 * TAIL)],
        in_specs=[pl.BlockSpec(memory_space=pltpu.VMEM), pl.BlockSpec(memory_space=pltpu.HBM)],
        out_specs=[pl.BlockSpec(memory_space=pltpu.VMEM)] * 2,
        scratch_shapes=[pltpu.VMEM((TAIL, size), jnp.float32), pltpu.SemaphoreType.DMA((2,))],
        compiler_params=pltpu.CompilerParams(vmem_limit_bytes=56 * 1024 * 1024),
        name="pack",
    )(pattern, flat)

    def columns_of(pieces):
        return jnp.concatenate([x[half : half + rows, :keep].astype(jnp.int32) for x in pieces], axis=0)

    def steps(part):
        up1 = fetched(part, -1, lambda z: z >= 1)
        down1 = fetched(part, 1, lambda z: z <= line - 2)
        up2 = fetched(up1, -1, lambda z: z >= 2)
        down2 = fetched(down1, 1, lambda z: z <= line - 3)
        brought_up, brought_down = up2, down2
        for step in range(3, line - 1):
            brought_up = fetched(brought_up, -1, lambda z: z >= step)
            brought_down = fetched(brought_down, 1, lambda z: z <= line - 1 - step)
        brought = jnp.where(z >= line - 2, brought_up, brought_down)
        total = line * lax.axis_size(("layer", "row"))
        over = [((i + line - 1) % total, i) for i in range(total) if i % line == line - 1]
        under = [((i + 1 - line) % total, i) for i in range(total) if i % line == 0]
        near = lax.ppermute(brought, AXES, over + under)
        over = [((i + line) % total, i) for i in range(total) if i % line >= line - 2]
        under = [((i - line) % total, i) for i in range(total) if i % line <= 1]
        far = lax.ppermute(brought, AXES, over + under)
        return (up1, up2, down1, down2), near, far

    line_a, near_a, far_a = steps(parts[0])
    line_b, near_b, far_b = steps(parts[1])

    group = row_at // rows
    known = ((group != 0) | (z >= 2)) & ((group != 1) | (z >= 1))
    known = known & ((group != 3) | (z <= line - 2)) & ((group != 4) | (z <= line - 3))
    up, down = columns_of([line_a[1], line_a[0]]), columns_of(line_a[2:])
    extended = jnp.concatenate([up, distance, down], axis=0)
    extended = jnp.where(known & (extended != UNUSED), extended + row_at, -1)
    hit = extended[:, :, None] == jnp.arange(span, dtype=jnp.int32)[None, None, :]
    flat_slot = jnp.arange(span * keep, dtype=jnp.int32).reshape(span, keep, 1)
    where_early = jnp.min(jnp.where(hit, flat_slot, span * keep), axis=1)
    columns = jnp.where(distance != UNUSED, distance + reach + row_at[:rows], -1)

    low = z <= 1
    late = columns_of([far_a, near_a, far_a])
    late = jnp.where(low, late[:reach], late[rows : rows + reach])
    group = row_at[:reach] // rows
    known = jnp.where(low, (group == 0) | (z == 0), jnp.where(group == 0, z == line - 1, z >= line - 2))
    first = jnp.where(low, 0, reach)
    late = jnp.where(known & (late != UNUSED), late + first + row_at[:reach], -1)
    hit = late[:, :, None] == jnp.arange(2 * reach, dtype=jnp.int32)[None, None, :]
    at = row_at[:reach]
    local = at // rows * (rows // 2) + at % (rows // 2)
    late_slot = local[:, :, None] * keep + jnp.arange(keep, dtype=jnp.int32)[None, :, None]
    where_late = jnp.min(jnp.where(hit, late_slot, rows * keep), axis=1)
    place = jnp.stack([z, jnp.int32(line)]).astype(jnp.int32)

    spread = jnp.repeat(jnp.eye(groups, dtype=jnp.bfloat16), 4, axis=1)
    factor = jnp.dot(pair_direction.reshape(3 * rows * keep * groups, groups), spread)
    factor = factor.reshape(3, rows, keep, groups, size)

    hbm = pl.BlockSpec(memory_space=pltpu.HBM)
    vmem = pl.BlockSpec(memory_space=pltpu.VMEM)
    smem = pl.BlockSpec(memory_space=pltpu.SMEM)
    limit = pltpu.CompilerParams(vmem_limit_bytes=60 * 1024 * 1024)
    mine = (atom_of_group[:, None] == jnp.arange(atoms, dtype=jnp.int32)[None, :]).astype(jnp.bfloat16)
    where_early, factor, mine = lax.optimization_barrier((where_early, factor, mine))
    mixture, left = pl.pallas_call(
        functools.partial(early_kernel, rows, keep),
        out_shape=(
            jax.ShapeDtypeStruct(density.shape, jnp.float32),
            jax.ShapeDtypeStruct((2, rows * size, rows * size), jnp.bfloat16),
        ),
        in_specs=[smem] * 3 + [hbm] * 9,
        out_specs=(hbm, hbm),
        scratch_shapes=[
            pltpu.VMEM(((span * keep + 1) * size, size), jnp.bfloat16),
            pltpu.VMEM((rows * size, span * size), jnp.bfloat16),
            pltpu.VMEM((span, rows * size, size), jnp.float32),
            pltpu.VMEM(density.shape, jnp.float32),
            pltpu.VMEM((2, rows * size, rows * size), jnp.bfloat16),
            pltpu.SemaphoreType.DMA((5, 2)),
            pltpu.SemaphoreType.DMA((rows + 1,)),
        ],
        compiler_params=limit,
        name="early",
    )(where_early, columns, place, flat, *[x for pair in zip(line_a, line_b) for x in pair])
    held_shape = ((rows * keep + 1) * size, size)
    square_shape = (2 * reach, rows * size, size)
    kept = [mixture, ham_derivative, factor, mine, left[1]]
    room = 60 * 1024 * 1024 - sum(x.size * x.dtype.itemsize for x in kept)
    kept = pl.pallas_call(
        functools.partial(middle_kernel, rows, keep),
        out_shape=[pltpu.VMEM(x.shape, x.dtype) for x in kept],
        in_specs=[smem] * 3 + [hbm] * 7,
        out_specs=[vmem] * 5,
        scratch_shapes=[
            pltpu.VMEM(left.shape[1:], left.dtype),
            pltpu.VMEM(held_shape, jnp.bfloat16),
            pltpu.VMEM(square_shape, jnp.float32),
            pltpu.SemaphoreType.DMA((3,)),
            pltpu.SemaphoreType.DMA((rows + 4,)),
        ],
        compiler_params=pltpu.CompilerParams(vmem_limit_bytes=room),
        name="middle",
    )(where_late, columns, place, left, near_a, far_a, mixture, ham_derivative, factor, mine)
    next_density, pieces = pl.pallas_call(
        functools.partial(late_kernel, rows, keep),
        out_shape=(
            jax.ShapeDtypeStruct(density.shape, density.dtype),
            jax.ShapeDtypeStruct((devices, 3, rows * groups), jnp.float32),
        ),
        in_specs=[smem] * 3 + [hbm] * 2 + [vmem] * 5,
        out_specs=(hbm, vmem),
        scratch_shapes=[
            pltpu.VMEM(held_shape, jnp.bfloat16),
            pltpu.VMEM(density.shape, density.dtype),
            pltpu.VMEM(square_shape, jnp.float32),
            pltpu.VMEM((size, size), jnp.float32),
            pltpu.VMEM((3, rows * groups, size), jnp.float32),
            pltpu.SemaphoreType.DMA((3,)),
            pltpu.SemaphoreType.DMA((rows,)),
        ],
        compiler_params=pltpu.CompilerParams(vmem_limit_bytes=32 * 1024 * 1024),
        name="late",
    )(where_late, columns, place, near_b, far_b, *kept)
    pieces = lax.all_to_all(pieces, AXES, split_axis=0, concat_axis=0, tiled=True)
    return next_density, jnp.sum(pieces, axis=0)


def solution(mesh):
    spread = P(AXES, None, None, None)
    return jax.shard_map(
        on_device,
        mesh=mesh,
        in_specs=(spread, P(AXES, None), spread, P(None, AXES, None, None), P(AXES)),
        out_specs=(spread, P(None, AXES)),
        check_vma=False,
    )
```

```python
import functools

import jax
import jax.numpy as jnp
from jax import lax
from jax.experimental import pallas as pl
from jax.experimental.pallas import tpu as pltpu
from jax.sharding import PartitionSpec as P

AXES = ("layer", "row", "col")
UNUSED = 64
TAIL = 16


def fetched(value, offset, keep):
    total = lax.axis_size(AXES)
    line = lax.axis_size("col")
    route = [((i + offset) % total, i) for i in range(total) if keep(i % line)]
    return lax.ppermute(value, AXES, route)


def pack_kernel(rows, blocks, pattern_ref, flat, first, second, wide, sems):
    half = flat.shape[0] // 2
    position = lax.axis_index(AXES)
    copies = [
        pltpu.make_async_copy(flat.at[pl.ds(n * half, half)], part.at[pl.ds(0, half)], sems.at[n])
        for n, part in enumerate((first, second))
    ]
    for copy in copies:
        copy.start()
    pattern = pattern_ref[...]
    reach = 2 * rows
    row = position * rows + lax.broadcasted_iota(jnp.int32, pattern.shape, 0)
    distance = lax.rem(pattern - row + (reach + blocks), blocks) - reach
    distance = jnp.where(pattern >= 0, distance, UNUSED)
    wide[...] = jnp.zeros_like(wide)
    wide[: pattern.shape[0], : pattern.shape[1]] = distance.astype(jnp.float32)
    first[pl.ds(half, TAIL)] = wide[...].astype(first.dtype)
    second[pl.ds(half, 2 * TAIL)] = jnp.zeros((2 * TAIL, second.shape[1]), second.dtype)
    for copy in copies:
        copy.wait()


def early_kernel(rows, keep, where_ref, column_ref, place_ref, own, *refs):
    near, (mixture_out, late_out, held, left, square, mixture_ref, late_ref, sems, out_sems) = refs[:8], refs[8:]
    near = [near[g : g + 2] for g in range(0, 8, 2)]
    size = own.shape[1]
    span = 5 * rows
    height = rows * keep * size
    half = height // 2
    z = place_ref[0]
    line = place_ref[1]
    sources = (
        (0, near[1], z >= 2),
        (1, near[0], z >= 1),
        (3, near[2], z <= line - 2),
        (4, near[3], z <= line - 3),
    )

    def copies(part, pair):
        return [
            pltpu.make_async_copy(
                pair[h].at[pl.ds(0, half)],
                held.at[pl.ds(part * height + h * half, half)],
                sems.at[part, h],
            )
            for h in range(2)
        ]

    mine = pltpu.make_async_copy(own, held.at[pl.ds(2 * height, height)], sems.at[2, 0])
    mine.start()
    for part, pair, valid in sources:

        @pl.when(valid)
        def _(part=part, pair=pair):
            for copy in copies(part, pair):
                copy.start()

    held[pl.ds(5 * height, size)] = jnp.zeros((size, size), held.dtype)
    left[...] = jnp.zeros(left.shape, left.dtype)
    mine.wait()
    for i in range(rows):
        for l in range(keep):
            column = column_ref[i, l]

            @pl.when(column >= 0)
            def _(i=i, l=l, column=column):
                at = pl.multiple_of(column * size, size)
                block = held[pl.ds(2 * height + (i * keep + l) * size, size)]
                left[i * size : (i + 1) * size, pl.ds(at, size)] = block

    width = late_ref.shape[2] // 2
    start = jnp.where(z <= 1, 0, span * size - 4 * width)
    for h in range(2):
        for part in range(2):
            at = pl.multiple_of(start + (2 * part + h) * width, size)
            late_ref[h, :, part * width : (part + 1) * width] = left[:, pl.ds(at, width)]
    put_left = pltpu.make_async_copy(late_ref, late_out, out_sems.at[rows])
    put_left.start()
    for part, pair, valid in sources:

        @pl.when(valid)
        def _(part=part, pair=pair):
            for copy in copies(part, pair):
                copy.wait()

    reach = 2 * rows
    for j in range(0, span, 2):
        low, high = max(0, j - reach), min(span, j + 2 + reach)

        def block(r, c):
            return held[pl.ds(pl.multiple_of(where_ref[r, c] * size, size), size)]

        right = jnp.concatenate(
            [jnp.concatenate([block(r, j), block(r, j + 1)], axis=1) for r in range(low, high)], axis=0
        )
        total = jnp.dot(left[:, low * size : high * size], right, preferred_element_type=jnp.float32)
        square[j] = total[:, :size]
        square[j + 1] = total[:, size:]

    put_mixture = []
    for i in range(rows):

        @pl.loop(0, keep, unroll=True)
        def _(k, i=i):
            column = column_ref[i, k]
            term = square[jnp.maximum(column, 0), i * size : (i + 1) * size, :]
            term = jnp.where(column >= 0, term, 0.0)
            at = pl.multiple_of(2 * height + (i * keep + k) * size, size)
            mixture_ref[i, k] = 2.0 * held[pl.ds(at, size)].astype(jnp.float32) - term

        put_mixture.append(pltpu.make_async_copy(mixture_ref.at[i], mixture_out.at[i], out_sems.at[i]))
        put_mixture[i].start()
    put_left.wait()
    for put in put_mixture:
        put.wait()


def late_terms(rows, keep, half, where_ref, place_ref, given, left, held, square, sems):
    left_in, near, far = given
    size = held.shape[1]
    reach = 2 * rows
    count = reach * keep * size // 4
    low = place_ref[0] <= 1
    near_at = pl.multiple_of(jnp.where(low, count, 0), size)
    far_at = pl.multiple_of(jnp.where(low, 0, count), size)
    gets = [
        pltpu.make_async_copy(far.at[pl.ds(0, count)], held.at[pl.ds(far_at, count)], sems.at[1]),
        pltpu.make_async_copy(near.at[pl.ds(0, count)], held.at[pl.ds(near_at, count)], sems.at[2]),
    ]
    if left_in is not None:
        gets.append(pltpu.make_async_copy(left_in.at[half], left, sems.at[0]))
    for get in gets:
        get.start()
    held[pl.ds(2 * count, size)] = jnp.zeros((size, size), held.dtype)

    def block(r, c):
        return held[pl.ds(pl.multiple_of(where_ref[r, c] * size, size), size)]

    def finish():
        for get in gets:
            get.wait()
        span = [part * rows + half * rows // 2 + n for part in range(2) for n in range(rows // 2)]
        for j in range(0, 2 * reach, 2):
            right = jnp.concatenate(
                [jnp.concatenate([block(r, j), block(r, j + 1)], axis=1) for r in span], axis=0
            )
            total = jnp.dot(left[...], right, preferred_element_type=jnp.float32)
            square[j] = total[:, :size]
            square[j + 1] = total[:, size:]

    def term(column, i):
        place = column - jnp.where(low, 0, rows)
        inside = (column >= 0) & (place >= 0) & (place < 2 * reach)
        value = square[jnp.where(inside, place, 0), i * size : (i + 1) * size, :]
        return jnp.where(inside, value, 0.0)

    return finish, term


def middle_kernel(
    rows, keep, where_ref, column_ref, place_ref, left_in, near, far, mixture_in, ham_in, factor_in, mine_in,
    mixture_ref, ham, factor, mine, left_out,
    left, held, square, sems, row_sems,
):
    given = (left_in, near, far)
    finish, term = late_terms(rows, keep, 0, where_ref, place_ref, given, left, held, square, sems)
    gets = [pltpu.make_async_copy(mixture_in.at[i], mixture_ref.at[i], row_sems.at[i]) for i in range(rows)]
    kept = [(ham_in, ham), (factor_in, factor), (mine_in, mine), (left_in.at[1], left_out)]
    others = [
        pltpu.make_async_copy(there, here, row_sems.at[rows + n]) for n, (there, here) in enumerate(kept)
    ]
    for get in gets + others:
        get.start()
    finish()
    for i in range(rows):
        gets[i].wait()

        @pl.loop(0, keep, unroll=True)
        def _(k, i=i):
            mixture_ref[i, k] = mixture_ref[i, k] - term(column_ref[i, k], i)

    for get in others:
        get.wait()


def late_kernel(
    rows, keep, where_ref, column_ref, place_ref, near, far, mixture_ref, ham_ref, factor_ref, mine, left,
    next_out, force_ref,
    held, next_ref, square, product, sums_ref, sems, out_sems,
):
    given = (None, near, far)
    finish, term = late_terms(rows, keep, 1, where_ref, place_ref, given, left, held, square, sems)
    size = ham_ref.shape[2]
    groups = size // 4
    puts = [pltpu.make_async_copy(next_ref.at[i], next_out.at[i], out_sems.at[i]) for i in range(rows)]
    finish()
    for i in range(rows):

        def slot(k, sums, i=i):
            mixture = mixture_ref[i, k] - term(column_ref[i, k], i)
            next_ref[i, k] = mixture.astype(next_ref.dtype)
            spot = product.at[k % 4]
            spot[...] = mixture * ham_ref[i, k].astype(jnp.float32)
            energy = spot[pl.ds(0, groups, stride=4), :]
            for r in range(1, 4):
                energy = energy + spot[pl.ds(r, groups, stride=4), :]
            return tuple(sums[d] + energy * factor_ref[d, i, k].astype(jnp.float32) for d in range(3))

        start = tuple(jnp.zeros((groups, size), jnp.float32) for _ in range(3))
        sums = start
        for k in range(keep):
            sums = slot(k, sums)
        puts[i].start()
        for d in range(3):
            sums_ref[d, i * groups : (i + 1) * groups] = sums[d]

    def split(value):
        high = value.astype(jnp.bfloat16)
        rest = value - high.astype(jnp.float32)
        middle = rest.astype(jnp.bfloat16)
        low = (rest - middle.astype(jnp.float32)).astype(jnp.bfloat16)
        return high, middle, low

    ones = jnp.ones((8, size), jnp.bfloat16)
    line = lax.broadcasted_iota(jnp.int32, (8, rows * groups), 0)
    force = jnp.zeros((8, rows * groups), jnp.float32)
    for d in range(3):
        total = sum(
            lax.dot_general(ones, part, (((1,), (1,)), ((), ())), preferred_element_type=jnp.float32)
            for part in split(sums_ref[d])
        )
        force = jnp.where(line == d, total, force)
    parts = jnp.concatenate([part.astype(jnp.float32) for part in split(force)], axis=0).astype(jnp.bfloat16)
    own_atoms = force_ref.shape[2]
    batch = 8

    def place(n, carry):
        at = pl.multiple_of(n * batch * own_atoms, own_atoms)
        placed = jnp.dot(parts, mine[:, pl.ds(at, batch * own_atoms)], preferred_element_type=jnp.float32)
        placed = placed[:8] + placed[8:16] + placed[16:]
        for e in range(batch):
            force_ref[n * batch + e] = placed[:3, e * own_atoms : (e + 1) * own_atoms]
        return carry

    lax.fori_loop(0, force_ref.shape[0] // batch, place, 0, unroll=True if force_ref.shape[0] <= 64 else 1)
    for put in puts:
        put.wait()


def on_device(density, pattern, ham_derivative, pair_direction, atom_of_group):
    rows, keep, size, _ = density.shape
    groups = size // 4
    devices = lax.axis_size(AXES)
    line = lax.axis_size("col")
    blocks = rows * devices
    atoms = blocks * groups
    reach = 2 * rows
    span = 5 * rows
    position = lax.axis_index(AXES)
    z = lax.axis_index("col")

    row_at = jnp.arange(span, dtype=jnp.int32)[:, None]
    distance = jnp.mod(pattern - (position * rows + row_at[:rows]) + reach, blocks) - reach
    distance = jnp.where(pattern >= 0, distance, UNUSED)
    flat = density.reshape(rows * keep * size, size)
    half = rows * keep * size // 2
    parts = pl.pallas_call(
        functools.partial(pack_kernel, rows, blocks),
        out_shape=[pltpu.VMEM((half + n, size), density.dtype) for n in (TAIL, 2 * TAIL)],
        in_specs=[pl.BlockSpec(memory_space=pltpu.VMEM), pl.BlockSpec(memory_space=pltpu.HBM)],
        out_specs=[pl.BlockSpec(memory_space=pltpu.VMEM)] * 2,
        scratch_shapes=[pltpu.VMEM((TAIL, size), jnp.float32), pltpu.SemaphoreType.DMA((2,))],
        compiler_params=pltpu.CompilerParams(vmem_limit_bytes=56 * 1024 * 1024),
        name="pack",
    )(pattern, flat)

    def columns_of(pieces):
        return jnp.concatenate([x[half : half + rows, :keep].astype(jnp.int32) for x in pieces], axis=0)

    def steps(part):
        up1 = fetched(part, -1, lambda z: z >= 1)
        down1 = fetched(part, 1, lambda z: z <= line - 2)
        up2 = fetched(up1, -1, lambda z: z >= 2)
        down2 = fetched(down1, 1, lambda z: z <= line - 3)
        brought_up, brought_down = up2, down2
        for step in range(3, line - 1):
            brought_up = fetched(brought_up, -1, lambda z: z >= step)
            brought_down = fetched(brought_down, 1, lambda z: z <= line - 1 - step)
        brought = jnp.where(z >= line - 2, brought_up, brought_down)
        brought = brought[: half + TAIL] if part is parts[0] else brought[:half]
        total = line * lax.axis_size(("layer", "row"))
        over = [((i + line - 1) % total, i) for i in range(total) if i % line == line - 1]
        under = [((i + 1 - line) % total, i) for i in range(total) if i % line == 0]
        near = lax.ppermute(brought, AXES, over + under)
        over = [((i + line) % total, i) for i in range(total) if i % line >= line - 2]
        under = [((i - line) % total, i) for i in range(total) if i % line <= 1]
        far = lax.ppermute(brought, AXES, over + under)
        return (up1, up2, down1, down2), near, far

    line_a, near_a, far_a = steps(parts[0])
    line_b, near_b, far_b = steps(parts[1])

    group = row_at // rows
    known = ((group != 0) | (z >= 2)) & ((group != 1) | (z >= 1))
    known = known & ((group != 3) | (z <= line - 2)) & ((group != 4) | (z <= line - 3))
    up, down = columns_of([line_a[1], line_a[0]]), columns_of(line_a[2:])
    extended = jnp.concatenate([up, distance, down], axis=0)
    extended = jnp.where(known & (extended != UNUSED), extended + row_at, -1)
    hit = extended[:, :, None] == jnp.arange(span, dtype=jnp.int32)[None, None, :]
    flat_slot = jnp.arange(span * keep, dtype=jnp.int32).reshape(span, keep, 1)
    where_early = jnp.min(jnp.where(hit, flat_slot, span * keep), axis=1)
    columns = jnp.where(distance != UNUSED, distance + reach + row_at[:rows], -1)

    low = z <= 1
    late = columns_of([far_a, near_a, far_a])
    late = jnp.where(low, late[:reach], late[rows : rows + reach])
    group = row_at[:reach] // rows
    known = jnp.where(low, (group == 0) | (z == 0), jnp.where(group == 0, z == line - 1, z >= line - 2))
    first = jnp.where(low, 0, reach)
    late = jnp.where(known & (late != UNUSED), late + first + row_at[:reach], -1)
    hit = late[:, :, None] == jnp.arange(2 * reach, dtype=jnp.int32)[None, None, :]
    at = row_at[:reach]
    local = at // rows * (rows // 2) + at % (rows // 2)
    late_slot = local[:, :, None] * keep + jnp.arange(keep, dtype=jnp.int32)[None, :, None]
    where_late = jnp.min(jnp.where(hit, late_slot, rows * keep), axis=1)
    place = jnp.stack([z, jnp.int32(line)]).astype(jnp.int32)

    spread = jnp.repeat(jnp.eye(groups, dtype=jnp.bfloat16), 4, axis=1)
    factor = jnp.dot(pair_direction.reshape(3 * rows * keep * groups, groups), spread)
    factor = factor.reshape(3, rows, keep, groups, size)

    hbm = pl.BlockSpec(memory_space=pltpu.HBM)
    vmem = pl.BlockSpec(memory_space=pltpu.VMEM)
    smem = pl.BlockSpec(memory_space=pltpu.SMEM)
    limit = pltpu.CompilerParams(vmem_limit_bytes=60 * 1024 * 1024)
    mine = (atom_of_group[:, None] == jnp.arange(atoms, dtype=jnp.int32)[None, :]).astype(jnp.bfloat16)
    where_early, factor, mine = lax.optimization_barrier((where_early, factor, mine))
    mixture, left = pl.pallas_call(
        functools.partial(early_kernel, rows, keep),
        out_shape=(
            jax.ShapeDtypeStruct(density.shape, jnp.float32),
            jax.ShapeDtypeStruct((2, rows * size, rows * size), jnp.bfloat16),
        ),
        in_specs=[smem] * 3 + [hbm] * 9,
        out_specs=(hbm, hbm),
        scratch_shapes=[
            pltpu.VMEM(((span * keep + 1) * size, size), jnp.bfloat16),
            pltpu.VMEM((rows * size, span * size), jnp.bfloat16),
            pltpu.VMEM((span, rows * size, size), jnp.float32),
            pltpu.VMEM(density.shape, jnp.float32),
            pltpu.VMEM((2, rows * size, rows * size), jnp.bfloat16),
            pltpu.SemaphoreType.DMA((5, 2)),
            pltpu.SemaphoreType.DMA((rows + 1,)),
        ],
        compiler_params=limit,
        name="early",
    )(where_early, columns, place, flat, *[x for pair in zip(line_a, line_b) for x in pair])
    held_shape = ((rows * keep + 1) * size, size)
    square_shape = (2 * reach, rows * size, size)
    kept = [mixture, ham_derivative, factor, mine, left[1]]
    room = 60 * 1024 * 1024 - sum(x.size * x.dtype.itemsize for x in kept)
    kept = pl.pallas_call(
        functools.partial(middle_kernel, rows, keep),
        out_shape=[pltpu.VMEM(x.shape, x.dtype) for x in kept],
        in_specs=[smem] * 3 + [hbm] * 7,
        out_specs=[vmem] * 5,
        scratch_shapes=[
            pltpu.VMEM(left.shape[1:], left.dtype),
            pltpu.VMEM(held_shape, jnp.bfloat16),
            pltpu.VMEM(square_shape, jnp.float32),
            pltpu.SemaphoreType.DMA((3,)),
            pltpu.SemaphoreType.DMA((rows + 4,)),
        ],
        compiler_params=pltpu.CompilerParams(vmem_limit_bytes=room),
        name="middle",
    )(where_late, columns, place, left, near_a, far_a, mixture, ham_derivative, factor, mine)
    next_density, pieces = pl.pallas_call(
        functools.partial(late_kernel, rows, keep),
        out_shape=(
            jax.ShapeDtypeStruct(density.shape, density.dtype),
            jax.ShapeDtypeStruct((devices, 3, rows * groups), jnp.float32),
        ),
        in_specs=[smem] * 3 + [hbm] * 2 + [vmem] * 5,
        out_specs=(hbm, vmem),
        scratch_shapes=[
            pltpu.VMEM(held_shape, jnp.bfloat16),
            pltpu.VMEM(density.shape, density.dtype),
            pltpu.VMEM(square_shape, jnp.float32),
            pltpu.VMEM((4, size, size), jnp.float32),
            pltpu.VMEM((3, rows * groups, size), jnp.float32),
            pltpu.SemaphoreType.DMA((3,)),
            pltpu.SemaphoreType.DMA((rows,)),
        ],
        compiler_params=pltpu.CompilerParams(vmem_limit_bytes=32 * 1024 * 1024),
        name="late",
    )(where_late, columns, place, near_b, far_b, *kept)
    pieces = lax.all_to_all(pieces, AXES, split_axis=0, concat_axis=0, tiled=True)
    return next_density, jnp.sum(pieces, axis=0)


def solution(mesh):
    spread = P(AXES, None, None, None)
    return jax.shard_map(
        on_device,
        mesh=mesh,
        in_specs=(spread, P(AXES, None), spread, P(None, AXES, None, None), P(AXES)),
        out_specs=(spread, P(None, AXES)),
        check_vma=False,
    )
```
